128 devices in a mesh: seq: 64 (over z, x, y), head: 2 (over core).
Axes of the slice: x: 4, y: 4, z: 4, core: 2. Of those that a mesh axis runs over, the one named last changes fastest.
Arguments:
- queries: bfloat16 [65536, 1024], P('seq', 'head'), may hold values from -8 to 8
- key_rows: bfloat16 [65536, 1024], P('seq', 'head'), may hold values from -8 to 8
- value_rows: bfloat16 [65536, 1024], P('seq', 'head'), may hold values from -6 to 6
- out_weight: bfloat16 [1024, 1024], P('head'), may hold values from -0.1875 to 0.1875
- cotangent: bfloat16 [65536, 1024], P('seq'), may hold values from -6 to 6
Outputs:
- mixed: bfloat16 [65536, 1024], P('seq', 'head')
- query_grad: bfloat16 [65536, 1024], P('seq', 'head')
- key_grad: bfloat16 [65536, 1024], P('seq', 'head')
- value_grad: bfloat16 [65536, 1024], P('seq', 'head')
- weight_grad: float32 [1024, 1024], P('head')
The draws below stay inside these ranges and needn't reach their ends.
All inputs are finite; a program needn't handle non-finite values.
Results may differ from the reference program's by a relative error of at most 0.02.
Values may be sent and summed in bfloat16 or wider, within the bound.
A program may use at most 256 MiB of HBM per device.

```python
import jax
import jax.numpy as jnp
from jax import lax

HEADS = 16
DH = 64
D = 1024
LANDMARKS = 256
ITERS = 2
TOKENS = 65536
SEGMENT = 256


def segment_means(key):
    means = jax.random.normal(key, (LANDMARKS, D), jnp.float32) * 0.9
    return jnp.broadcast_to(means[:, None, :], (LANDMARKS, SEGMENT, D)).reshape(TOKENS, D)


def draw_queries(key, part):
    means = segment_means(key)
    key = jax.random.fold_in(key, 11)
    values = means + jax.random.normal(key, (TOKENS, D), jnp.float32)
    return jnp.clip(values, -8.0, 8.0).astype(jnp.bfloat16)


def draw_key_rows(key, part):
    means = segment_means(key)
    key = jax.random.fold_in(key, 13)
    values = means + jax.random.normal(key, (TOKENS, D), jnp.float32)
    return jnp.clip(values, -8.0, 8.0).astype(jnp.bfloat16)


def level_of(rng, dims, pieces, low, high):
    def one(dim, blocks):
        draws = jax.random.uniform(jax.random.fold_in(jax.random.fold_in(rng, 6), dim), (blocks,), jnp.float32, low / len(pieces), high / len(pieces))
        return jnp.repeat(jnp.exp(draws), dims[dim] // blocks).reshape((-1,) + (1,) * (len(dims) - dim - 1))

    loudness = one(*pieces[0])
    for cut in pieces[1:]:
        loudness = loudness * one(*cut)
    return loudness


def gaussian(rng, shape, spread, bound, cuts=(), kind=jnp.bfloat16):
    drawn = spread * jax.random.normal(rng, shape, jnp.float32)
    if cuts:
        drawn = drawn * level_of(rng, shape, cuts, -0.22, 0.18)
    return jnp.clip(drawn, -bound, bound).astype(kind)


def setup_inputs(seed: int = 0) -> dict:
    splits = jax.random.split(jax.random.key(seed), 6)
    return {
        "queries": draw_queries(jax.random.fold_in(splits[5], 71), 0),
        "key_rows": draw_key_rows(jax.random.fold_in(splits[5], 71), 0),
        "value_rows": gaussian(splits[2], (TOKENS, D), 1.0, 6.0, ((0, 64), (1, 2))),
        "out_weight": gaussian(splits[3], (D, D), D ** -0.5, 0.1875, ((0, 2),)),
        "cotangent": gaussian(splits[4], (TOKENS, D), 1.0, 6.0, ((0, 64),)),
    }


softmax_scale_factor = 0.125

def product_high(left, right):
    return jnp.dot(left, right, precision=lax.Precision.HIGHEST)

def pseudo_inverse(amat):
    column_top = lax.stop_gradient(jnp.max(lax.optimization_barrier(jnp.sum(amat, axis=0))))
    current = amat.T / column_top
    ident = jnp.eye(amat.shape[0], dtype=amat.dtype)
    for iteration in range(ITERS):
        apply_z = product_high(amat, current)
        inner = 7.0 * ident - apply_z
        inner = 15.0 * ident - product_high(apply_z, inner)
        inner = 13.0 * ident - product_high(apply_z, inner)
        current = 0.25 * product_high(current, inner)
    return current

def one_head(query_h, key_h, value_h, grad_h):
    float_single = jnp.float32
    bf16 = jnp.bfloat16
    landmark_queries = lax.optimization_barrier(jnp.mean(query_h.astype(float_single).reshape(LANDMARKS, SEGMENT, DH), axis=1)).astype(bf16)
    landmark_keys = lax.optimization_barrier(jnp.mean(key_h.astype(float_single).reshape(LANDMARKS, SEGMENT, DH), axis=1)).astype(bf16)
    kernel_f = jax.nn.softmax(jnp.dot(query_h, landmark_keys.T, preferred_element_type=float_single) * softmax_scale_factor, axis=1)
    kernel_fb = kernel_f.astype(bf16)
    scores_b = jnp.dot(landmark_queries, key_h.T, preferred_element_type=float_single) * softmax_scale_factor
    weights_p = jnp.exp(scores_b - lax.optimization_barrier(jnp.max(scores_b, axis=1, keepdims=True)))
    totals = lax.optimization_barrier(jnp.sum(weights_p, axis=1, keepdims=True))
    weights_pb = weights_p.astype(bf16)
    landmark_value_rows = jnp.dot(weights_pb, value_h, preferred_element_type=float_single) / totals
    kernel_a = jax.nn.softmax(jnp.dot(landmark_queries, landmark_keys.T, preferred_element_type=float_single) * softmax_scale_factor, axis=1)
    approximate_inverse, pull_back = jax.vjp(pseudo_inverse, kernel_a)
    mixing_matrix = product_high(approximate_inverse, landmark_value_rows)
    mixer_b = mixing_matrix.astype(bf16)
    attn_h = jnp.dot(kernel_fb, mixer_b, preferred_element_type=float_single).astype(bf16)
    mixing_matrix_gradient = jnp.dot(kernel_fb.T, grad_h, preferred_element_type=float_single)
    grad_f = jnp.dot(grad_h, mixer_b.T, preferred_element_type=float_single)
    grad_sf = (kernel_f * (grad_f - lax.optimization_barrier(jnp.sum(kernel_f * grad_f, axis=1, keepdims=True)))).astype(bf16)
    query_f = jnp.dot(grad_sf, landmark_keys, preferred_element_type=float_single) * softmax_scale_factor
    land_k_f = jnp.dot(grad_sf.T, query_h, preferred_element_type=float_single) * softmax_scale_factor
    inverse_matrix_gradient = product_high(mixing_matrix_gradient, landmark_value_rows.T)
    landmark_value_gradient = product_high(approximate_inverse.T, mixing_matrix_gradient)
    grad_a = pull_back(inverse_matrix_gradient)[0]
    query_kernel_gradient = kernel_a * (grad_a - lax.optimization_barrier(jnp.sum(kernel_a * grad_a, axis=1, keepdims=True)))
    landmark_query_kernel = product_high(query_kernel_gradient, landmark_keys.astype(float_single)) * softmax_scale_factor
    landmark_key_kernel = product_high(query_kernel_gradient.T, landmark_queries.astype(float_single)) * softmax_scale_factor
    grad_norm = landmark_value_gradient / totals
    grad_norm_b = grad_norm.astype(bf16)
    center = lax.optimization_barrier(jnp.sum(grad_norm * landmark_value_rows, axis=1, keepdims=True))
    grad_sb = (weights_p * (jnp.dot(grad_norm_b, value_h.T, preferred_element_type=float_single) - center)).astype(bf16)
    land_q_b = jnp.dot(grad_sb, key_h, preferred_element_type=float_single) * softmax_scale_factor
    key_b = jnp.dot(grad_sb.T, landmark_queries, preferred_element_type=float_single) * softmax_scale_factor
    value_out = jnp.dot(weights_pb.T, grad_norm_b, preferred_element_type=float_single).astype(bf16)
    land_q_all = land_q_b + landmark_query_kernel
    land_k_all = land_k_f + landmark_key_kernel
    query_out = (query_f + jnp.repeat(land_q_all / SEGMENT, SEGMENT, axis=0)).astype(bf16)
    key_out = (key_b + jnp.repeat(land_k_all / SEGMENT, SEGMENT, axis=0)).astype(bf16)
    return (attn_h, query_out, key_out, value_out)

def reference(queries, key_rows, value_rows, out_weight, cotangent):
    grad_attn = jnp.dot(cotangent, out_weight.T, preferred_element_type=jnp.float32).astype(jnp.bfloat16)

    def split_heads(array):
        return array.reshape(TOKENS, HEADS, DH).transpose(1, 0, 2)

    def join_heads(array):
        return array.transpose(1, 0, 2).reshape(TOKENS, D)
    attn, query_grad, key_grad, value_grad = lax.map(lambda items: one_head(items[0], items[1], items[2], items[3]), (split_heads(queries), split_heads(key_rows), split_heads(value_rows), split_heads(grad_attn)))
    attn = join_heads(attn)
    mixed = jnp.dot(attn, out_weight, preferred_element_type=jnp.float32).astype(jnp.bfloat16)
    weight_grad = jnp.dot(attn.T, cotangent, preferred_element_type=jnp.float32)
    return (mixed, join_heads(query_grad), join_heads(key_grad), join_heads(value_grad), weight_grad)
```

```python
import jax
import jax.numpy as jnp
from jax import lax
from jax.experimental import pallas as pl
from jax.experimental.pallas import tpu as pltpu
from jax.sharding import PartitionSpec as P

MESH = pl.DeviceIdType.MESH


def exchange_body(n, gather, x_ref, o_ref, send_sem, recv_sem, own_sem):
    me = lax.axis_index("seq")
    barrier = pltpu.get_barrier_semaphore()

    def greet(d, carry):
        pl.semaphore_signal(
            barrier, inc=1, device_id={"seq": lax.rem(me + d, n)}, device_id_type=MESH
        )
        return carry

    lax.fori_loop(1, n, greet, 0)
    pl.semaphore_wait(barrier, n - 1)
    own = pltpu.make_async_copy(x_ref if gather else x_ref.at[me], o_ref.at[me], own_sem)
    own.start()

    def send(d, carry):
        to = lax.rem(me + d, n)
        pltpu.make_async_remote_copy(
            src_ref=x_ref if gather else x_ref.at[to],
            dst_ref=o_ref.at[me],
            send_sem=send_sem,
            recv_sem=recv_sem,
            device_id={"seq": to},
            device_id_type=MESH,
        ).start()
        return carry

    lax.fori_loop(1, n, send, 0)
    own.wait()
    rest = o_ref.at[pl.ds(0, n - 1)]
    pltpu.make_async_copy(rest, rest, recv_sem).wait()
    pltpu.make_async_copy(rest, rest, send_sem).wait()


def exchange(x, collective, gather=False):
    n = lax.axis_size("seq")
    shape = (n,) + x.shape if gather else x.shape
    return pl.pallas_call(
        lambda *refs: exchange_body(n, gather, *refs),
        out_shape=jax.ShapeDtypeStruct(shape, x.dtype),
        in_specs=[pl.BlockSpec(memory_space=pltpu.VMEM)],
        out_specs=pl.BlockSpec(memory_space=pltpu.VMEM),
        scratch_shapes=[pltpu.SemaphoreType.DMA] * 3,
        compiler_params=pltpu.CompilerParams(
            collective_id=collective, has_side_effects=True, vmem_limit_bytes=48 * 2**20
        ),
    )(x)

DH = 64
LANDMARKS = 256
ITERS = 2


softmax_scale_factor = 0.125


def batched_precise_product(spec, left, right):
    return jnp.einsum(spec, left, right, precision=lax.Precision.HIGHEST)


def pseudo_inverse(amat):
    column_top = lax.stop_gradient(jnp.max(jnp.sum(amat, axis=1), axis=-1))
    current = jnp.swapaxes(amat, 1, 2) / column_top[:, None, None]
    ident = jnp.eye(amat.shape[1], dtype=amat.dtype)
    for iteration in range(ITERS):
        apply_z = batched_precise_product("hij,hjk->hik", amat, current)
        inner = 7.0 * ident - apply_z
        inner = 15.0 * ident - batched_precise_product("hij,hjk->hik", apply_z, inner)
        inner = 13.0 * ident - batched_precise_product("hij,hjk->hik", apply_z, inner)
        current = 0.25 * batched_precise_product("hij,hjk->hik", current, inner)
    return current


def local(queries, key_rows, value_rows, out_weight, cotangent):
    float_single = jnp.float32
    bf16 = jnp.bfloat16
    row_count, columns = queries.shape
    local_heads = columns // DH
    land_dev = LANDMARKS // lax.axis_size("seq")
    seg_len = row_count // land_dev
    own_start = lax.axis_index("seq") * land_dev
    grad_attn = jnp.dot(cotangent, out_weight.T, preferred_element_type=float_single).astype(bf16)
    own_q = jnp.mean(
        queries.astype(float_single).reshape(land_dev, seg_len, columns), axis=1
    ).astype(bf16)
    own_k = jnp.mean(
        key_rows.astype(float_single).reshape(land_dev, seg_len, columns), axis=1
    ).astype(bf16)
    own_both = jnp.concatenate([own_q, own_k], axis=0).reshape(-1, 256)
    landmarks = exchange(own_both, 1, gather=True).reshape(-1, 2, land_dev, columns)
    landmark_queries = landmarks[:, 0]
    landmark_keys = landmarks[:, 1]
    landmark_queries = landmark_queries.reshape(LANDMARKS, local_heads, DH)
    landmark_keys = landmark_keys.reshape(LANDMARKS, local_heads, DH)
    query_heads = queries.reshape(row_count, local_heads, DH)
    key_heads = key_rows.reshape(row_count, local_heads, DH)
    value_heads = value_rows.reshape(row_count, local_heads, DH)
    grad_heads = grad_attn.reshape(row_count, local_heads, DH)
    kernel_f = jax.nn.softmax(
        jnp.einsum("thd,lhd->thl", query_heads, landmark_keys, preferred_element_type=float_single)
        * softmax_scale_factor,
        axis=-1,
    )
    kernel_fb = kernel_f.astype(bf16)
    scores_b = (
        jnp.einsum("lhd,thd->hlt", landmark_queries, key_heads, preferred_element_type=float_single)
        * softmax_scale_factor
    )
    own_top = jnp.max(scores_b, axis=-1)
    top = jnp.max(exchange(own_top, 2, gather=True), axis=0)[..., None]
    weights_p = jnp.exp(scores_b - top)
    weights_pb = weights_p.astype(bf16)
    partial_values = jnp.einsum(
        "hlt,thd->hld", weights_pb, value_heads, preferred_element_type=float_single
    )
    own_total = jnp.sum(weights_p, axis=-1)
    totals = jnp.sum(exchange(own_total, 3, gather=True), axis=0)[..., None]
    sums = jnp.sum(exchange(partial_values.reshape(-1, 16, 128), 4), axis=0)
    summed = exchange(sums, 5, gather=True).reshape(partial_values.shape)
    landmark_value_rows = summed / totals
    kernel_a = jax.nn.softmax(
        jnp.einsum(
            "jtq,itq->tji", landmark_queries, landmark_keys, preferred_element_type=float_single
        )
        * softmax_scale_factor,
        axis=-1,
    )
    approximate_inverse, pull_back = jax.vjp(pseudo_inverse, kernel_a)
    mixing_matrix = batched_precise_product(
        "yzc,ycw->yzw", approximate_inverse, landmark_value_rows
    )
    mixer_b = mixing_matrix.astype(bf16)
    attn_flat = (
        jnp.einsum("thl,hld->thd", kernel_fb, mixer_b, preferred_element_type=float_single)
        .astype(bf16)
        .reshape(row_count, columns)
    )
    partial_out = jnp.dot(attn_flat, out_weight, preferred_element_type=float_single)
    mixed = (
        lax.psum_scatter(partial_out.astype(jnp.bfloat16), "head", scatter_dimension=1, tiled=True)
        .astype(jnp.float32)
        .astype(bf16)
    )
    weight_part = jnp.dot(attn_flat.T, cotangent, preferred_element_type=float_single)
    weight_sum = jnp.sum(
        exchange(weight_part.astype(bf16).reshape(-1, 16, 512), 6).astype(float_single), axis=0
    )
    weight_grad = (
        exchange(weight_sum.astype(bf16), 7, gather=True)
        .astype(float_single)
        .reshape(weight_part.shape)
    )
    local_mixer_grad = jnp.einsum(
        "thl,thd->hld", kernel_fb, grad_heads, preferred_element_type=float_single
    )
    grad_f = jnp.einsum("thd,hld->thl", grad_heads, mixer_b, preferred_element_type=float_single)
    grad_sf = (kernel_f * (grad_f - jnp.sum(kernel_f * grad_f, axis=-1, keepdims=True))).astype(
        bf16
    )
    query_f = (
        jnp.einsum("thl,lhd->thd", grad_sf, landmark_keys, preferred_element_type=float_single)
        * softmax_scale_factor
    )
    land_k_f = (
        jnp.einsum("thl,thd->lhd", grad_sf, query_heads, preferred_element_type=float_single)
        * softmax_scale_factor
    )
    mixer_sums = jnp.sum(exchange(local_mixer_grad.reshape(-1, 16, 128), 8), axis=0)
    mixing_matrix_gradient = exchange(mixer_sums, 9, gather=True).reshape(local_mixer_grad.shape)
    inverse_matrix_gradient = batched_precise_product(
        "pae,pse->pas", mixing_matrix_gradient, landmark_value_rows
    )
    landmark_value_gradient = batched_precise_product(
        "zer,zeq->zrq", approximate_inverse, mixing_matrix_gradient
    )
    grad_a = pull_back(inverse_matrix_gradient)[0]
    query_kernel_gradient = kernel_a * (grad_a - jnp.sum(kernel_a * grad_a, axis=-1, keepdims=True))
    landmark_query_kernel = (
        batched_precise_product(
            "pgz,zpe->gpe", query_kernel_gradient, landmark_keys.astype(float_single)
        )
        * softmax_scale_factor
    )
    landmark_key_kernel = (
        batched_precise_product(
            "kjg,jki->gki", query_kernel_gradient, landmark_queries.astype(float_single)
        )
        * softmax_scale_factor
    )
    grad_norm = landmark_value_gradient / totals
    grad_norm_b = grad_norm.astype(bf16)
    center = jnp.sum(grad_norm * landmark_value_rows, axis=-1, keepdims=True)
    grad_sb = (
        weights_p
        * (
            jnp.einsum(
                "hld,thd->hlt", grad_norm_b, value_heads, preferred_element_type=float_single
            )
            - center
        )
    ).astype(bf16)
    land_q_b = (
        jnp.einsum("hlt,thd->lhd", grad_sb, key_heads, preferred_element_type=float_single)
        * softmax_scale_factor
    )
    key_b = (
        jnp.einsum("hlt,lhd->thd", grad_sb, landmark_queries, preferred_element_type=float_single)
        * softmax_scale_factor
    )
    value_grad = (
        jnp.einsum("hlt,hld->thd", weights_pb, grad_norm_b, preferred_element_type=float_single)
        .astype(bf16)
        .reshape(row_count, columns)
    )
    both = jnp.concatenate(
        [land_q_b.reshape(-1, 16, 128), land_k_f.reshape(-1, 16, 128)], axis=1
    )
    both = jnp.sum(exchange(both, 10), axis=0)
    own_q_grad = both[:16].reshape(land_dev, local_heads, DH)
    own_k_grad = both[16:].reshape(land_dev, local_heads, DH)
    own_q_grad = own_q_grad + lax.dynamic_slice_in_dim(
        landmark_query_kernel, own_start, land_dev, 0
    )
    own_k_grad = own_k_grad + lax.dynamic_slice_in_dim(landmark_key_kernel, own_start, land_dev, 0)
    spread_q = (own_q_grad / seg_len).reshape(land_dev, 1, columns)
    spread_k = (own_k_grad / seg_len).reshape(land_dev, 1, columns)
    query_grad = (
        (query_f.reshape(land_dev, seg_len, columns) + spread_q)
        .astype(bf16)
        .reshape(row_count, columns)
    )
    key_grad = (
        (key_b.reshape(land_dev, seg_len, columns) + spread_k)
        .astype(bf16)
        .reshape(row_count, columns)
    )
    return (mixed, query_grad, key_grad, value_grad, weight_grad)


def solution(mesh):
    return jax.shard_map(
        local,
        mesh=mesh,
        in_specs=(
            P("seq", "head"),
            P("seq", "head"),
            P("seq", "head"),
            P("head", None),
            P("seq", None),
        ),
        out_specs=(
            P("seq", "head"),
            P("seq", "head"),
            P("seq", "head"),
            P("seq", "head"),
            P("head", None),
        ),
        check_vma=False,
    )
```
